32 devices in a mesh: group: 2 (over x), shard: 16 (over z, y, core).
Axes of the slice: x: 2, y: 2, z: 4, core: 2. Of those that a mesh axis runs over, the one named last changes fastest.
Arguments:
- replica_weights: bfloat16 [2, 16, 512, 2048], P('group', None, 'shard'), may hold values from -6 to 6
- anchor_slabs: float32 [16, 2, 512, 2048], P('shard', None, None, 'group'), may hold values from -6 to 6
- momentum_slabs: float32 [16, 2, 512, 2048], P('shard', None, None, 'group'), may hold values from -4 to 4
- slab_owner: int32 [16], replicated, may hold values from 0 to 15, as said below
- replica_embed: bfloat16 [2, 768, 512], P('group', 'shard'), may hold values from -6 to 6
- anchor_embed: float32 [768, 512], P('shard'), may hold values from -6 to 6
- momentum_embed: float32 [768, 512], P('shard'), may hold values from -4 to 4
- embed_basis: float32 [768, 64], P('shard'), may hold values from -0.21875 to 0.21875
Outputs:
- new_anchor_slabs: float32 [16, 2, 512, 2048], P('shard', None, None, 'group')
- new_momentum_slabs: float32 [16, 2, 512, 2048], P('shard', None, None, 'group')
- new_weights: bfloat16 [2, 16, 512, 2048], P('group', None, 'shard')
- new_anchor_embed: float32 [768, 512], P('shard')
- new_momentum_embed: float32 [768, 512], P('shard')
- new_embed_weights: bfloat16 [2, 768, 512], P('group', 'shard')
The draws below stay inside these ranges and needn't reach their ends.
Inputs may be any that keep to these rules, and one draw needn't show every extreme that they name: `slab_owner`: of the devices of shard, a quarter own 2 matrices each, half own 1 each and a quarter own none.
All inputs are finite; a program needn't handle non-finite values.
Results may differ from the reference program's by a relative error of at most 0.008.
Values may be sent and summed in bfloat16 or wider, within the bound.
No kernel may reach another device: no remote copies, remote signals or barrier semaphores. Data moves between devices by JAX's collectives and lax.ppermute only.
A program may use at most 128 MiB of HBM per device.

```python
import jax
import jax.numpy as jnp
from jax import lax

D = 512
FF = 2048
PATCH = 768
RANK = 64
SLABS_DEV = 1
CAP = 2
NSLAB = 16
N_GROUP = 2
N_SHARD = 16


def draw_slab_owner(key, part):
    devices = NSLAB // SLABS_DEV
    quarter = devices // 4
    order_key = jax.random.fold_in(key, 11)
    shuffle_key = jax.random.fold_in(key, 23)
    device_order = jax.random.permutation(order_key, devices).astype(jnp.int32)
    heavy_owners = jnp.repeat(device_order[:quarter], CAP)
    middle_owners = jnp.repeat(device_order[quarter:3 * quarter], SLABS_DEV)
    owners = jnp.concatenate([heavy_owners, middle_owners]).astype(jnp.int32)
    slab_order = jax.random.permutation(shuffle_key, NSLAB).astype(jnp.int32)
    return jnp.take(owners, slab_order).astype(jnp.int32)


def levels(own_key, shape, cuts, smallest, largest):
    def one(dim, parts):
        draws = jax.random.uniform(jax.random.fold_in(jax.random.fold_in(own_key, 6), dim), (parts,), jnp.float32, smallest / len(cuts), largest / len(cuts))
        return jnp.repeat(jnp.exp(draws), shape[dim] // parts).reshape((-1,) + (1,) * (len(shape) - dim - 1))

    gain = one(*cuts[0])
    for cut in cuts[1:]:
        gain = gain * one(*cut)
    return gain


def bell_draw(stream_key, dims, deviation, most, shards=(), kind=jnp.bfloat16):
    array = deviation * jax.random.normal(stream_key, dims, jnp.float32)
    if shards:
        array = array * levels(stream_key, dims, shards, -0.22, 0.18)
    return jnp.clip(array, -most, most).astype(kind)


def setup_inputs(seed: int = 0) -> dict:
    seeds = jax.random.split(jax.random.key(seed), 9)
    return {
        "replica_weights": bell_draw(seeds[0], (N_GROUP, NSLAB, D, FF), 1.0, 6.0, ((0, 2), (2, 16))),
        "anchor_slabs": bell_draw(seeds[1], (N_SHARD, CAP, D, FF), 1.0, 6.0, ((0, 16), (3, 2)), jnp.float32),
        "momentum_slabs": bell_draw(seeds[2], (N_SHARD, CAP, D, FF), 0.5, 4.0, ((0, 16), (3, 2)), jnp.float32),
        "slab_owner": draw_slab_owner(jax.random.fold_in(seeds[8], 71), 0),
        "replica_embed": bell_draw(seeds[4], (N_GROUP, PATCH, D), 1.0, 6.0, ((0, 2), (1, 16))),
        "anchor_embed": bell_draw(seeds[5], (PATCH, D), 1.0, 6.0, ((0, 16),), jnp.float32),
        "momentum_embed": bell_draw(seeds[6], (PATCH, D), 0.5, 4.0, ((0, 16),), jnp.float32),
        "embed_basis": bell_draw(seeds[7], (PATCH, RANK), PATCH ** -0.5, 0.21875, ((0, 16),), jnp.float32),
    }


OUTER_RATE = 0.7
MOMENTUM_COEF = 0.9


def slot_tables(slab_owner, devices, capacity):
    slab_count = slab_owner.shape[0]
    order_ids = jnp.arange(slab_count, dtype=jnp.int32)
    same_owner = slab_owner[:, None] == slab_owner[None, :]
    earlier = order_ids[None, :] < order_ids[:, None]
    slot_index = jnp.sum((same_owner & earlier).astype(jnp.int32), axis=1).astype(jnp.int32)
    matches = (slab_owner[:, None, None] == jnp.arange(devices, dtype=jnp.int32)[None, :, None]) & (slot_index[:, None, None] == jnp.arange(capacity, dtype=jnp.int32)[None, None, :])
    slab_of = jnp.sum(jnp.where(matches, order_ids[:, None, None], 0), axis=0).astype(jnp.int32)
    slot_used = jnp.any(matches, axis=0)
    return slot_index, slab_of, slot_used


def nesterov(anchor_value, moment, mean_value):
    outer_grad = anchor_value - mean_value
    new_moment = MOMENTUM_COEF * moment + outer_grad
    new_anchor = anchor_value - OUTER_RATE * (outer_grad + MOMENTUM_COEF * new_moment)
    return new_anchor, new_moment


def reference(replica_weights, anchor_slabs, momentum_slabs, slab_owner, replica_embed, anchor_embed, momentum_embed, embed_basis):
    devices = anchor_slabs.shape[0]
    capacity = anchor_slabs.shape[1]
    slot_index, slab_of, slot_used = slot_tables(slab_owner, devices, capacity)

    def per_device(items):
        anchor_here, moment_here, slab_ids, used_here = items
        picked = jnp.take(replica_weights, slab_ids, axis=1).astype(jnp.float32)
        mean_rows = jnp.sum(picked, axis=0) / N_GROUP
        new_anchor, new_moment = nesterov(anchor_here, moment_here, mean_rows)
        keep = used_here[:, None, None]
        return jnp.where(keep, new_anchor, anchor_here), jnp.where(keep, new_moment, moment_here)

    new_anchor_slabs, new_momentum_slabs = lax.map(per_device, (anchor_slabs, momentum_slabs, slab_of, slot_used))
    chosen = new_anchor_slabs[slab_owner, slot_index].astype(jnp.bfloat16)
    new_weights = jnp.broadcast_to(chosen[None], (N_GROUP,) + chosen.shape)

    mean_embed = jnp.sum(replica_embed.astype(jnp.float32), axis=0) / N_GROUP
    embed_factor = jnp.dot(embed_basis.T, anchor_embed - mean_embed, precision=lax.Precision.HIGHEST)
    embed_grad = jnp.dot(embed_basis, embed_factor, precision=lax.Precision.HIGHEST)
    new_anchor_embed, new_momentum_embed = nesterov(anchor_embed, momentum_embed, anchor_embed - embed_grad)
    embed_cast = new_anchor_embed.astype(jnp.bfloat16)
    new_embed_weights = jnp.broadcast_to(embed_cast[None], (N_GROUP,) + embed_cast.shape)
    return new_anchor_slabs, new_momentum_slabs, new_weights, new_anchor_embed, new_momentum_embed, new_embed_weights
```

```python
import jax
import jax.numpy as jnp
from jax import lax
from jax.experimental import pallas as pl
from jax.experimental.pallas import tpu as pltpu
from jax.sharding import PartitionSpec as P

OUTER_RATE = 0.7
MOMENTUM_COEF = 0.9
CHUNKS = 2
ROW_BLOCK = 128


def slot_tables(slab_owner, devices, capacity):
    slab_count = slab_owner.shape[0]
    order_ids = jnp.arange(slab_count, dtype=jnp.int32)
    same_owner = slab_owner[:, None] == slab_owner[None, :]
    earlier = order_ids[None, :] < order_ids[:, None]
    slot_index = jnp.sum((same_owner & earlier).astype(jnp.int32), axis=1)
    matches = (slab_owner[:, None, None] == jnp.arange(devices, dtype=jnp.int32)[None, :, None]) & (
        slot_index[:, None, None] == jnp.arange(capacity, dtype=jnp.int32)[None, None, :]
    )
    slab_of = jnp.sum(jnp.where(matches, order_ids[:, None, None], 0), axis=0)
    slot_used = jnp.any(matches, axis=0)
    return (slot_index, slab_of, slot_used)


def nesterov(anchor_value, moment, mean_value):
    outer_grad = anchor_value - mean_value
    new_moment = MOMENTUM_COEF * moment + outer_grad
    new_anchor = anchor_value - OUTER_RATE * (outer_grad + MOMENTUM_COEF * new_moment)
    return (new_anchor, new_moment)


def update_kernel(used_ref, got_ref, anchor_ref, moment_ref, *refs):
    new_anchor_ref, new_moment_ref, back_ref = refs[-3:]
    used = used_ref[pl.program_id(0)] > 0
    anchor = anchor_ref[0]
    moment = moment_ref[0]
    got = got_ref[...].astype(jnp.float32)
    mean = got.reshape(anchor.shape) * 0.5
    new_anchor, new_moment = nesterov(anchor, moment, mean)
    new_anchor = jnp.where(used, new_anchor, anchor)
    new_anchor_ref[0] = new_anchor
    new_moment_ref[0] = jnp.where(used, new_moment, moment)
    back_ref[...] = new_anchor.reshape(back_ref.shape).astype(back_ref.dtype)


def update_chunk(chunk, used, got, anchor, moment, earlier):
    devices, capacity, row_count, chunk_width = got.shape
    group_rows = ROW_BLOCK // row_count
    steps = devices // group_rows
    state = pl.BlockSpec((1, ROW_BLOCK, chunk_width), lambda c, i, *_: (c, i, chunk))
    parts = pl.BlockSpec((group_rows, None, row_count, chunk_width), lambda c, i, *_: (i, c, 0, 0))
    whole = pl.BlockSpec(memory_space=pl.ANY)
    aliases = {4: 0, 5: 1} if earlier else {}
    return pl.pallas_call(
        update_kernel,
        grid_spec=pltpu.PrefetchScalarGridSpec(
            num_scalar_prefetch=1,
            grid=(capacity, steps),
            in_specs=[parts, state, state] + [whole] * len(earlier),
            out_specs=[state, state, parts],
        ),
        out_shape=[
            jax.ShapeDtypeStruct(anchor.shape, anchor.dtype),
            jax.ShapeDtypeStruct(moment.shape, moment.dtype),
            jax.ShapeDtypeStruct(got.shape, got.dtype),
        ],
        input_output_aliases=aliases,
        compiler_params=pltpu.CompilerParams(vmem_limit_bytes=32 * 1024 * 1024),
    )(used, got, anchor, moment, *earlier)


def on_device(
    replica_weights,
    anchor_slabs,
    momentum_slabs,
    slab_owner,
    replica_embed,
    anchor_embed,
    momentum_embed,
    embed_basis,
):
    local_rows = replica_weights[0]
    slab_count, row_count, width = local_rows.shape
    devices = lax.axis_size("shard")
    n_group = lax.axis_size("group")
    capacity = anchor_slabs.shape[1]
    half = width // n_group
    chunk_width = half // CHUNKS
    group_here = lax.axis_index("group")
    swap = [(0, 1), (1, 0)]
    slot_index, slab_of, slot_used = slot_tables(slab_owner, devices, capacity)
    send_ids = slab_of.reshape(-1)
    back_ids = slab_owner * capacity + slot_index
    my_used = lax.dynamic_index_in_dim(
        slot_used, lax.axis_index("shard"), 0, keepdims=False
    ).astype(jnp.int32)

    def columns(column_group, chunk):
        start = column_group * half + chunk * chunk_width
        return lax.dynamic_slice_in_dim(local_rows, start, chunk_width, axis=2)

    peer_embed = lax.ppermute(replica_embed[0], "group", swap)
    peer_rows = [
        lax.ppermute(columns(1 - group_here, chunk), "group", swap) for chunk in range(CHUNKS)
    ]
    got = []
    for chunk in range(CHUNKS):
        mine = columns(group_here, chunk).astype(jnp.float32)
        summed = (mine + peer_rows[chunk].astype(jnp.float32)).astype(jnp.bfloat16)
        packed = jnp.take(summed, send_ids, axis=0)
        packed = packed.reshape(devices, capacity, row_count, chunk_width)
        got.append(lax.all_to_all(packed, "shard", split_axis=0, concat_axis=0, tiled=True))

    embed_sum = replica_embed[0].astype(jnp.float32) + peer_embed.astype(jnp.float32)
    partial_factor = jnp.dot(
        embed_basis.T, anchor_embed - embed_sum / n_group, precision=lax.Precision.HIGHEST
    )
    rank, embed_width = partial_factor.shape
    pieces = lax.all_to_all(
        partial_factor.reshape(devices, rank // devices, embed_width),
        "shard",
        split_axis=0,
        concat_axis=0,
        tiled=True,
    )
    piece = jnp.sum(pieces, axis=0, keepdims=True)
    embed_factor = lax.all_to_all(
        jnp.broadcast_to(piece, pieces.shape), "shard", split_axis=0, concat_axis=0, tiled=True
    ).reshape(rank, embed_width)

    state = ()
    received = []
    for chunk in range(CHUNKS):
        new_anchor, new_moment, back = update_chunk(
            chunk, my_used, got[chunk], anchor_slabs[0], momentum_slabs[0], state
        )
        state = (new_anchor, new_moment)
        received.append(lax.all_to_all(back, "shard", split_axis=0, concat_axis=0, tiled=True))
    new_rows = jnp.zeros((slab_count, row_count, width), jnp.bfloat16)
    for chunk in range(CHUNKS):
        flat = received[chunk].reshape(devices * capacity, row_count, chunk_width)
        own = jnp.take(flat, back_ids, axis=0)
        other = lax.ppermute(own, "group", swap)
        for column_group, value in ((group_here, own), (1 - group_here, other)):
            start = column_group * half + chunk * chunk_width
            new_rows = lax.dynamic_update_slice_in_dim(new_rows, value, start, axis=2)

    embed_grad = jnp.dot(embed_basis, embed_factor, precision=lax.Precision.HIGHEST)
    new_anchor_embed, new_momentum_embed = nesterov(
        anchor_embed, momentum_embed, anchor_embed - embed_grad
    )
    new_embed_rows = new_anchor_embed.astype(jnp.bfloat16)
    return (
        state[0][None],
        state[1][None],
        new_rows[None],
        new_anchor_embed,
        new_momentum_embed,
        new_embed_rows[None],
    )


def solution(mesh):
    in_specs = (
        P("group", None, "shard", None),
        P("shard", None, None, "group"),
        P("shard", None, None, "group"),
        P(),
        P("group", "shard", None),
        P("shard", None),
        P("shard", None),
        P("shard", None),
    )
    out_specs = (
        P("shard", None, None, "group"),
        P("shard", None, None, "group"),
        P("group", None, "shard", None),
        P("shard", None),
        P("shard", None),
        P("group", "shard", None),
    )
    return jax.shard_map(
        on_device, mesh=mesh, in_specs=in_specs, out_specs=out_specs, check_vma=False
    )
```

```python
import jax
import jax.numpy as jnp
from jax import lax
from jax.experimental import pallas as pl
from jax.experimental.pallas import tpu as pltpu
from jax.sharding import PartitionSpec as P

OUTER_RATE = 0.7
MOMENTUM_COEF = 0.9
PLANES = 4
CHUNKS = ((4, 2, False), (0, 4, False), (6, 2, False))
EMBED = None
ORDER = (
    (0, 0), (EMBED, 0), (1, 0), (2, 0), (EMBED, 0), (0, 1), (EMBED, 0), (1, 1, 0), (0, 2), (EMBED, 0),
    (0, 3), (2, 1, 1), (1, 2), (0, 4, 2), (2, 2), (1, 3), (EMBED, 0), (2, 3), (0, 5), (1, 4), (EMBED, 0),
    (2, 4, 1), (1, 5), (EMBED, 0), (0, 6), (2, 5), (1, 6), (2, 6),
)
VMEM_LIMIT = 48 * 1024 * 1024


def nesterov(anchor_value, moment, mean_value):
    outer_grad = anchor_value - mean_value
    new_moment = MOMENTUM_COEF * moment + outer_grad
    new_anchor = anchor_value - OUTER_RATE * (outer_grad + MOMENTUM_COEF * new_moment)
    return (new_anchor, new_moment)


def call(
    kernel, scalars, operands, in_specs, out_shape, out_specs, grid=(1,), aliases=None, after=(), name=None,
    scratch=()
):
    first, last = len(scalars), len(scalars) + len(after)

    def body(*refs):
        kernel(*refs[:first], *refs[last:])

    return pl.pallas_call(
        body,
        grid_spec=pltpu.PrefetchScalarGridSpec(
            num_scalar_prefetch=first,
            grid=grid,
            in_specs=[pl.BlockSpec(memory_space=pl.ANY)] * len(after) + in_specs,
            out_specs=out_specs,
            scratch_shapes=scratch,
        ),
        out_shape=out_shape,
        input_output_aliases={first + len(after) + i: o for i, o in (aliases or {}).items()},
        compiler_params=pltpu.CompilerParams(vmem_limit_bytes=VMEM_LIMIT),
        name=name,
        cost_estimate=pl.CostEstimate(flops=1, bytes_accessed=1, transcendentals=0),
    )(*scalars, *after, *operands)


def full(shape):
    return pl.BlockSpec(memory_space=pltpu.VMEM)


def like(shape, dtype=jnp.bfloat16):
    return jax.ShapeDtypeStruct(shape, dtype)


WHOLE = pl.BlockSpec(memory_space=pl.ANY)


def columns(group, rows, start, width):
    first = group * (rows.shape[2] // 2) + start
    return pl.ds(pl.multiple_of(first, width), width)


def take_columns(here, local_rows, start, width, after):
    block = local_rows.shape[:2] + (width,)

    def kernel(here_ref, rows_ref, *refs):
        done = refs[-1]
        copies = []
        for i, group in enumerate((1 - here_ref[0], here_ref[0])):
            chosen = columns(group, rows_ref, start, width)
            copies.append(pltpu.make_async_copy(rows_ref.at[:, :, chosen], refs[i], done.at[i]))
        for copy in copies:
            copy.start()
        for copy in copies:
            copy.wait()

    return call(
        kernel,
        (here,),
        (local_rows,),
        [WHOLE],
        [like(block)] * 2,
        [full(block)] * 2,
        after=after,
        scratch=[pltpu.SemaphoreType.DMA((2,))],
        name="take_columns",
    )


def sum_and_pack(plane_ids, mine, peer, slots, after):
    def kernel(ids_ref, mine_ref, peer_ref, *outs):
        for k, out in enumerate(outs):

            @pl.loop(0, slots)
            def _(j, k=k, out=out):
                i = ids_ref[k, j]
                out[j] = mine_ref[i] + peer_ref[i]

    packed = (slots,) + mine.shape[1:]
    return call(
        kernel,
        (plane_ids,),
        (mine, peer),
        [full(mine.shape)] * 2,
        [like(packed)] * PLANES,
        [full(packed)] * PLANES,
        after=after,
        name="sum_and_pack",
    )


def sum_for_owners(slab_of, mine, peer, after):
    devices, capacity = slab_of.shape

    def kernel(ids_ref, mine_ref, peer_ref, out):
        @pl.loop(0, devices)
        def _(d):
            for c in range(capacity):
                i = ids_ref[d, c]
                out[d, c] = mine_ref[i] + peer_ref[i]

    packed = (devices, capacity) + mine.shape[1:]
    return call(
        kernel,
        (slab_of,),
        (mine, peer),
        [full(mine.shape)] * 2,
        like(packed),
        full(packed),
        after=after,
        name="sum_for_owners",
    )


def pack_for_owners(here, owner_pos, parts, inside, capacity, after):
    slots, row_count, width = parts[0].shape

    def kernel(here_ref, pos_ref, *refs):
        ins, outs = refs[:PLANES], refs[PLANES:]
        for k, part in enumerate(ins):
            z = lax.rem(here_ref[1] + PLANES - k, PLANES)
            for m, out in enumerate(outs):
                for c in range(capacity):
                    out[c, z] = part[pos_ref[m, c]]

    packed = (capacity, PLANES, row_count, width)
    return call(
        kernel,
        (here, owner_pos),
        parts,
        [full(parts[0].shape)] * PLANES,
        [like(packed)] * inside,
        [full(packed)] * inside,
        after=after,
        name="pack_for_owners",
    )


def update_chunk(here, used, got, anchor, moment, start, earlier, after):
    capacity, planes, row_count, width = got[0].shape
    inside = len(got)

    def kernel(here_ref, used_ref, *refs):
        ins, anchor_ref, moment_ref = refs[:inside], refs[inside], refs[inside + 1]
        new_anchor_ref, new_moment_ref = refs[-inside - 2], refs[-inside - 1]
        outs = refs[-inside:]
        c = pl.program_id(0)
        used_here = used_ref[c] > 0

        @pl.loop(0, planes)
        def _(z):
            for m in range(inside):
                first = (z * inside + (here_ref[2] ^ m)) * row_count
                rows = pl.ds(pl.multiple_of(first, row_count), row_count)
                anchor_value = anchor_ref[rows, :]
                moment_value = moment_ref[rows, :]
                mean = ins[m][c, z].astype(jnp.float32) * 0.5
                new_anchor, new_moment = nesterov(anchor_value, moment_value, mean)
                new_anchor = jnp.where(used_here, new_anchor, anchor_value)
                new_anchor_ref[rows, :] = new_anchor
                new_moment_ref[rows, :] = jnp.where(used_here, new_moment, moment_value)
                outs[m][c, z] = new_anchor.astype(outs[m].dtype)

    state = pl.BlockSpec((None, anchor.shape[1], width), lambda c, *_: (c, 0, start // width))
    part = full(got[0].shape)
    return call(
        kernel,
        (here, used),
        (*got, anchor, moment, *earlier),
        [part] * inside + [state, state] + [WHOLE] * len(earlier),
        [like(anchor.shape, anchor.dtype)] * 2 + [like(got[0].shape)] * inside,
        [state, state] + [part] * inside,
        grid=(capacity,),
        aliases={inside + 2: 0, inside + 3: 1} if earlier else {},
        after=after,
        name="update_chunk",
    )


def update_owned(here, used, got, anchor, moment, start, earlier, after):
    devices, capacity, row_count, width = got.shape

    def kernel(here_ref, used_ref, got_ref, anchor_ref, moment_ref, *refs):
        new_anchor_ref, new_moment_ref, out_ref = refs[-3:]
        c = pl.program_id(0)
        used_here = used_ref[c] > 0

        @pl.loop(0, devices)
        def _(d):
            rows = pl.ds(pl.multiple_of(d * row_count, row_count), row_count)
            anchor_value = anchor_ref[rows, :]
            moment_value = moment_ref[rows, :]
            mean = got_ref[d, c].astype(jnp.float32) * 0.5
            new_anchor, new_moment = nesterov(anchor_value, moment_value, mean)
            new_anchor = jnp.where(used_here, new_anchor, anchor_value)
            new_anchor_ref[rows, :] = new_anchor
            new_moment_ref[rows, :] = jnp.where(used_here, new_moment, moment_value)
            out_ref[d, c] = new_anchor.astype(out_ref.dtype)

    state = pl.BlockSpec((None, anchor.shape[1], width), lambda c, *_: (c, 0, start // width))
    part = full(got.shape)
    return call(
        kernel,
        (here, used),
        (got, anchor, moment, *earlier),
        [part, state, state] + [WHOLE] * len(earlier),
        [like(anchor.shape, anchor.dtype)] * 2 + [like(got.shape)],
        [state, state, part],
        grid=(capacity,),
        aliases={3: 0, 4: 1} if earlier else {},
        after=after,
        name="update_owned",
    )


def pack_for_planes(here, owner_pos, owner_used, backs, slots, after):
    capacity, _, row_count, width = backs[0].shape
    inside = len(backs)

    def kernel(here_ref, pos_ref, used_ref, *refs):
        ins, outs = refs[:inside], refs[inside:]
        for m in range(inside):
            for c in range(capacity):

                @pl.when(used_ref[m, c] > 0)
                def _(m=m, c=c):
                    for k, out in enumerate(outs):
                        out[pos_ref[m, c]] = ins[m][c, lax.rem(here_ref[1] + k, PLANES)]

    packed = (slots, row_count, width)
    return call(
        kernel,
        (here, owner_pos, owner_used),
        backs,
        [full(backs[0].shape)] * inside,
        [like(packed)] * PLANES,
        [full(packed)] * PLANES,
        after=after,
        name="pack_for_planes",
    )


def unpack(in_ids, in_counts, parts, slab_count, after):
    _, row_count, width = parts[0].shape

    def kernel(ids_ref, counts_ref, *refs):
        for k in range(PLANES):

            @pl.loop(0, counts_ref[k])
            def _(j, k=k):
                refs[-1][ids_ref[k, j]] = refs[k][j]

    block = (slab_count, row_count, width)
    return call(
        kernel,
        (in_ids, in_counts),
        parts,
        [full(parts[0].shape)] * PLANES,
        like(block),
        full(block),
        after=after,
        name="unpack",
    )


def unpack_owned(slab_owner, slot_index, got, after):
    slab_count = slab_owner.shape[0]

    def kernel(owner_ref, slot_ref, got_ref, out_ref):
        @pl.loop(0, slab_count)
        def _(s):
            out_ref[s] = got_ref[owner_ref[s], slot_ref[s]]

    block = (slab_count,) + got.shape[2:]
    return call(
        kernel,
        (slab_owner, slot_index),
        (got,),
        [full(got.shape)],
        like(block),
        full(block),
        after=after,
        name="unpack_owned",
    )


def place(here, own, other, start, whole_shape, earlier, after):
    width = own.shape[2]

    def kernel(here_ref, own_ref, other_ref, *refs):
        out_ref, done = refs[-2:]
        copies = []
        for i, (group, value) in enumerate(((here_ref[0], own_ref), (1 - here_ref[0], other_ref))):
            chosen = columns(group, out_ref, start, width)
            copies.append(pltpu.make_async_copy(value, out_ref.at[:, :, chosen], done.at[i]))
        for copy in copies:
            copy.start()
        for copy in copies:
            copy.wait()

    return call(
        kernel,
        (here,),
        (own, other, *earlier),
        [full(own.shape)] * 2 + [WHOLE] * len(earlier),
        like(whole_shape),
        WHOLE,
        aliases={2: 0} if earlier else {},
        after=after,
        scratch=[pltpu.SemaphoreType.DMA((2,))],
        name="place",
    )


def project_embed(embed_basis, anchor_embed, embed_rows, peer_rows, after):
    def kernel(basis_ref, anchor_ref, mine_ref, peer_ref, out_ref):
        total = mine_ref[...].astype(jnp.float32) + peer_ref[...].astype(jnp.float32)
        out_ref[...] = lax.dot_general(
            basis_ref[...],
            anchor_ref[...] - total * 0.5,
            (((0,), (0,)), ((), ())),
            precision=lax.Precision.HIGHEST,
            preferred_element_type=jnp.float32,
        )

    operands = (embed_basis, anchor_embed, embed_rows, peer_rows)
    shape = (embed_basis.shape[1], anchor_embed.shape[1])
    return call(
        kernel,
        (),
        operands,
        [full(value.shape) for value in operands],
        like(shape, jnp.float32),
        full(shape),
        after=after,
        name="project_embed",
    )


def add(first, second, after):
    def kernel(first_ref, second_ref, out_ref):
        out_ref[...] = first_ref[...] + second_ref[...]

    return call(
        kernel,
        (),
        (first, second),
        [full(first.shape)] * 2,
        like(first.shape, first.dtype),
        full(first.shape),
        after=after,
        name="add",
    )


def update_embed(embed_basis, embed_factor, anchor_embed, momentum_embed, after):
    def kernel(basis_ref, factor_ref, anchor_ref, moment_ref, *outs):
        embed_grad = jnp.dot(
            basis_ref[...],
            factor_ref[...],
            precision=lax.Precision.HIGHEST,
            preferred_element_type=jnp.float32,
        )
        anchor = anchor_ref[...]
        new_anchor, new_moment = nesterov(anchor, moment_ref[...], anchor - embed_grad)
        for out, value in zip(outs, (new_anchor, new_moment, new_anchor)):
            out[...] = value.astype(out.dtype)

    operands = (embed_basis, embed_factor, anchor_embed, momentum_embed)
    shape = anchor_embed.shape
    return call(
        kernel,
        (),
        operands,
        [full(value.shape) for value in operands],
        [like(shape, jnp.float32), like(shape, jnp.float32), like(shape)],
        [full(shape)] * 3,
        after=after,
        name="update_embed",
    )


def moved(
    slots,
    tables,
    local_rows,
    anchor,
    moment,
    embed_rows,
    anchor_embed,
    momentum_embed,
    embed_basis,
):
    (here, to_ids, from_ids, from_counts, owner_pos, owner_used, my_used, slab_of, slab_owner,
        slot_index) = tables
    devices = lax.axis_size("shard")
    inside = devices // PLANES
    capacity = anchor.shape[0]
    eighth = local_rows.shape[2] // 16
    swap = [(0, 1), (1, 0)]
    def over_planes(parts):
        return [parts[0]] + [
            lax.ppermute(
                parts[k], "shard", [(i, (i + k * inside) % devices) for i in range(devices)]
            )
            for k in range(1, PLANES)
        ]

    def over_devices(value):
        return lax.all_to_all(value, "shard", split_axis=0, concat_axis=0, tiled=True)

    def in_plane(parts):
        return [parts[0]] + [
            lax.ppermute(parts[m], "shard", [(i, i ^ m) for i in range(devices)])
            for m in range(1, inside)
        ]

    def embed_steps():
        after = yield None
        rows = lax.optimization_barrier((embed_rows, *after))[0]
        peer = lax.ppermute(rows, "group", swap)
        after = yield after[0]
        factor = project_embed(embed_basis, anchor_embed, embed_rows, peer, after)
        step = 1
        while step < devices:
            pairs = [(i, i ^ step) for i in range(devices)]
            other = lax.ppermute(factor, "shard", pairs)
            after = yield factor
            factor = add(factor, other, after)
            step *= 2
        after = yield factor
        yield update_embed(embed_basis, factor, anchor_embed, momentum_embed, after)

    embed = embed_steps()
    next(embed)
    new_embed = None
    held = [None] * len(CHUNKS)
    state, new_rows, after = (), (), ()
    for chunk, step, *waits in ORDER:
        for wait in waits:
            after += tuple(held[wait])
        if chunk == EMBED:
            new_embed = embed.send(after)
            if isinstance(new_embed, jax.Array):
                after = (new_embed,)
            continue
        start, width, direct = CHUNKS[chunk]
        start, width = start * eighth, width * eighth
        value = held[chunk]
        if step == 0:
            if not after:
                first = (1 - here[0]) * (local_rows.shape[2] // 2) + start
                after = (lax.dynamic_slice_in_dim(local_rows, first, width, axis=2),)
                value = lax.ppermute(after[0], "group", swap)
                token, mine = take_columns(here, local_rows, start, width, after)
                value = (mine, value)
            else:
                token, mine = take_columns(here, local_rows, start, width, after)
                value = (mine, lax.ppermute(token, "group", swap))
        elif step == 1 and direct:
            token = sum_for_owners(slab_of, *value, after)
            value = over_devices(token)
        elif step == 1:
            parts = sum_and_pack(to_ids, *value, slots, after)
            token, value = parts[0], over_planes(parts)
        elif step == 2:
            parts = pack_for_owners(here, owner_pos, value, inside, capacity, after)
            token = parts[0]
            value = in_plane(parts)
        elif step == 3 and direct:
            *state, token = update_owned(here, my_used, value, anchor, moment, start, state, after)
            value = over_devices(token)
        elif step == 3:
            first, second, *parts = update_chunk(
                here, my_used, value, anchor, moment, start, state, after
            )
            state, token, value = (first, second), parts[0], in_plane(parts)
        elif step == 4:
            parts = pack_for_planes(here, owner_pos, owner_used, value, slots, after)
            token, value = parts[0], over_planes(parts)
        elif step == 5:
            if direct:
                token = unpack_owned(slab_owner, slot_index, value, after)
            else:
                token = unpack(from_ids, from_counts, value, slab_owner.shape[0], after)
            value = (token, lax.ppermute(token, "group", swap))
        else:
            new_rows = (place(here, *value, start, local_rows.shape, new_rows, after),)
        held[chunk] = value
        after = (token,)
    while isinstance(new_embed, jax.Array):
        new_embed = embed.send(after)
    return (*state, *new_rows, *new_embed)


def on_device(
    replica_weights,
    anchor_slabs,
    momentum_slabs,
    slab_owner,
    replica_embed,
    anchor_embed,
    momentum_embed,
    embed_basis,
):
    slab_count = slab_owner.shape[0]
    devices = lax.axis_size("shard")
    capacity = anchor_slabs.shape[1]
    inside = devices // PLANES
    device_here = lax.axis_index("shard")
    plane, place_here = device_here // inside, device_here % inside
    here = jnp.stack([lax.axis_index("group"), plane, place_here]).astype(jnp.int32)

    order = jnp.arange(slab_count, dtype=jnp.int32)
    earlier = order[None, :] < order[:, None]
    same_owner = slab_owner[:, None] == slab_owner[None, :]
    slab_plane = slab_owner // inside
    same_plane = slab_plane[:, None] == slab_plane[None, :]
    slot_index = jnp.sum((same_owner & earlier).astype(jnp.int32), axis=1)
    position = jnp.sum((same_plane & earlier).astype(jnp.int32), axis=1)
    offsets = jnp.arange(PLANES, dtype=jnp.int32)
    places = jnp.arange(capacity * inside, dtype=jnp.int32)

    def slots_of(planes):
        held = slab_plane[None, :] == planes[:, None]
        at_place = held[:, None, :] & (position[None, None, :] == places[None, :, None])
        return (
            jnp.sum(jnp.where(at_place, order, 0), axis=2),
            jnp.sum(held.astype(jnp.int32), axis=1),
        )

    to_ids, _ = slots_of((plane + offsets) % PLANES)
    from_ids, from_counts = slots_of((plane - offsets) % PLANES)
    owners = plane * inside + (place_here ^ jnp.arange(inside, dtype=jnp.int32))
    at_owner = (slab_owner[None, None, :] == owners[:, None, None]) & (
        slot_index[None, None, :] == jnp.arange(capacity, dtype=jnp.int32)[None, :, None]
    )
    owner_pos = jnp.sum(jnp.where(at_owner, position, 0), axis=2)
    owner_used = jnp.any(at_owner, axis=2).astype(jnp.int32)
    matches = (slab_owner[None, None, :] == jnp.arange(devices, dtype=jnp.int32)[:, None, None]) & (
        slot_index[None, None, :] == jnp.arange(capacity, dtype=jnp.int32)[None, :, None]
    )
    slab_of = jnp.sum(jnp.where(matches, order, 0), axis=2)
    tables = (
        here, to_ids, from_ids, from_counts, owner_pos, owner_used, owner_used[0], slab_of, slab_owner, slot_index
    )

    most = capacity * inside
    fewer = most * 3 // 4
    operands = (
        tables,
        replica_weights[0],
        anchor_slabs[0],
        momentum_slabs[0],
        replica_embed[0],
        anchor_embed,
        momentum_embed,
        embed_basis,
    )
    results = lax.cond(
        jnp.max(from_counts) <= fewer,
        lambda *values: moved(fewer, *values),
        lambda *values: moved(most, *values),
        *operands,
    )
    return tuple(
        value[None] if index not in (3, 4) else value for index, value in enumerate(results)
    )


def solution(mesh):
    in_specs = (
        P("group", None, "shard", None),
        P("shard", None, None, "group"),
        P("shard", None, None, "group"),
        P(),
        P("group", "shard", None),
        P("shard", None),
        P("shard", None),
        P("shard", None),
    )
    out_specs = (
        P("shard", None, None, "group"),
        P("shard", None, None, "group"),
        P("group", None, "shard", None),
        P("shard", None),
        P("shard", None),
        P("group", "shard", None),
    )
    return jax.shard_map(
        on_device, mesh=mesh, in_specs=in_specs, out_specs=out_specs, check_vma=False
    )
```

```python
import jax
import jax.numpy as jnp
from jax import lax
from jax.experimental import pallas as pl
from jax.experimental.pallas import tpu as pltpu
from jax.sharding import PartitionSpec as P

OUTER_RATE = 0.7
MOMENTUM_COEF = 0.9
PLANES = 4
CHUNKS = ((4, 2), (0, 4), (6, 2))
EMBED = None
FIRST = 0
ORDER = (
    (0, 1), (1, 1, 0), (0, 2), (EMBED, 0), (0, 3), (EMBED, 0), (2, 1, 1), (1, 2), (EMBED, 0),
    (0, 4, 2), (2, 2), (1, 3), (2, 3), (0, 5), (1, 4), (2, 4, 1), (EMBED, 0), (1, 5), (0, 6), (2, 5), (EMBED, 0),
    (1, 6), (EMBED, 0), (2, 6),
)
VMEM_LIMIT = 48 * 1024 * 1024


def nesterov(anchor_value, moment, mean_value):
    outer_grad = anchor_value - mean_value
    new_moment = MOMENTUM_COEF * moment + outer_grad
    new_anchor = anchor_value - OUTER_RATE * (outer_grad + MOMENTUM_COEF * new_moment)
    return (new_anchor, new_moment)


def call(
    kernel, scalars, operands, in_specs, out_shape, out_specs, grid=(1,), aliases=None, after=(), name=None,
    scratch=()
):
    first, last = len(scalars), len(scalars) + len(after)

    def body(*refs):
        kernel(*refs[:first], *refs[last:])

    return pl.pallas_call(
        body,
        grid_spec=pltpu.PrefetchScalarGridSpec(
            num_scalar_prefetch=first,
            grid=grid,
            in_specs=[pl.BlockSpec(memory_space=pl.ANY)] * len(after) + in_specs,
            out_specs=out_specs,
            scratch_shapes=scratch,
        ),
        out_shape=out_shape,
        input_output_aliases={first + len(after) + i: o for i, o in (aliases or {}).items()},
        compiler_params=pltpu.CompilerParams(vmem_limit_bytes=VMEM_LIMIT),
        name=name,
        cost_estimate=pl.CostEstimate(flops=1, bytes_accessed=1, transcendentals=0),
    )(*scalars, *after, *operands)


def full(shape):
    return pl.BlockSpec(memory_space=pltpu.VMEM)


def like(shape, dtype=jnp.bfloat16):
    return jax.ShapeDtypeStruct(shape, dtype)


WHOLE = pl.BlockSpec(memory_space=pl.ANY)


def columns(group, rows, start, width):
    first = group * (rows.shape[2] // 2) + start
    return pl.ds(pl.multiple_of(first, width), width)


def slot_tables(here, slab_owner, devices, capacity):
    inside = devices // PLANES
    slab_count = slab_owner.shape[0]
    plane_slots = capacity * inside
    shift = inside.bit_length() - 1

    def kernel(
        here_ref, owner_ref, to_ref, from_ref, count_ref, pos_ref, used_ref, most_ref, planes, owners
    ):
        plane, place_here = here_ref[1], here_ref[2]
        for k in range(PLANES):
            planes[k] = 0

            @pl.loop(0, plane_slots)
            def _(j, k=k):
                to_ref[k, j] = 0
                from_ref[k, j] = 0

        @pl.loop(0, devices)
        def _(o):
            owners[o] = 0

        @pl.loop(0, inside)
        def _(m):
            for c in range(capacity):
                pos_ref[m, c] = 0
                used_ref[m, c] = 0

        @pl.loop(0, slab_count)
        def _(s):
            owner = owner_ref[s]
            its_plane = owner >> shift
            j, c = planes[its_plane], owners[owner]
            planes[its_plane] = j + 1
            owners[owner] = c + 1
            to_ref[(its_plane - plane) & (PLANES - 1), j] = s
            from_ref[(plane - its_plane) & (PLANES - 1), j] = s

            @pl.when(its_plane == plane)
            def _():
                m = (owner & (inside - 1)) ^ place_here
                pos_ref[m, c] = j
                used_ref[m, c] = 1

        most = planes[0]
        for k in range(PLANES):
            count_ref[k] = planes[(plane - k) & (PLANES - 1)]
            most = jnp.maximum(most, planes[k])
        most_ref[0] = most

    shapes = [(PLANES, plane_slots)] * 2 + [(PLANES,)] + [(inside, capacity)] * 2 + [(1,)]
    scalars = pl.BlockSpec(memory_space=pltpu.SMEM)
    return call(
        kernel,
        (here, slab_owner),
        (),
        [],
        [like(shape, jnp.int32) for shape in shapes],
        [scalars] * len(shapes),
        scratch=[pltpu.SMEM((PLANES,), jnp.int32), pltpu.SMEM((devices,), jnp.int32)],
        name="slot_tables",
    )


def sum_and_pack(plane_ids, mine, peer, slots, after):
    def kernel(ids_ref, mine_ref, peer_ref, *outs):
        for k, out in enumerate(outs):

            @pl.loop(0, slots)
            def _(j, k=k, out=out):
                i = ids_ref[k, j]
                out[j] = mine_ref[i] + peer_ref[i]

    packed = (slots,) + mine.shape[1:]
    return call(
        kernel,
        (plane_ids,),
        (mine, peer),
        [full(mine.shape)] * 2,
        [like(packed)] * PLANES,
        [full(packed)] * PLANES,
        after=after,
        name="sum_and_pack",
    )


def pack_for_owners(here, owner_pos, parts, inside, capacity, after):
    slots, row_count, width = parts[0].shape

    def kernel(here_ref, pos_ref, *refs):
        ins, outs = refs[:PLANES], refs[PLANES:]
        for k, part in enumerate(ins):
            z = lax.rem(here_ref[1] + PLANES - k, PLANES)
            for m, out in enumerate(outs):
                for c in range(capacity):
                    out[c, z] = part[pos_ref[m, c]]

    packed = (capacity, PLANES, row_count, width)
    return call(
        kernel,
        (here, owner_pos),
        parts,
        [full(parts[0].shape)] * PLANES,
        [like(packed)] * inside,
        [full(packed)] * inside,
        after=after,
        name="pack_for_owners",
    )


def update_chunk(here, used, got, anchor, moment, start, earlier, after):
    capacity, planes, row_count, width = got[0].shape
    inside = len(got)

    def kernel(here_ref, used_ref, *refs):
        ins, anchor_ref, moment_ref = refs[:inside], refs[inside], refs[inside + 1]
        new_anchor_ref, new_moment_ref = refs[-inside - 2], refs[-inside - 1]
        outs = refs[-inside:]
        c = pl.program_id(0)
        used_here = used_ref[0, c] > 0

        @pl.loop(0, planes)
        def _(z):
            for m in range(inside):
                first = (z * inside + (here_ref[2] ^ m)) * row_count
                rows = pl.ds(pl.multiple_of(first, row_count), row_count)
                anchor_value = anchor_ref[rows, :]
                moment_value = moment_ref[rows, :]
                mean = ins[m][c, z].astype(jnp.float32) * 0.5
                new_anchor, new_moment = nesterov(anchor_value, moment_value, mean)
                new_anchor = jnp.where(used_here, new_anchor, anchor_value)
                new_anchor_ref[rows, :] = new_anchor
                new_moment_ref[rows, :] = jnp.where(used_here, new_moment, moment_value)
                outs[m][c, z] = new_anchor.astype(outs[m].dtype)

    state = pl.BlockSpec((None, anchor.shape[1], width), lambda c, *_: (c, 0, start // width))
    part = full(got[0].shape)
    return call(
        kernel,
        (here, used),
        (*got, anchor, moment, *earlier),
        [part] * inside + [state, state] + [WHOLE] * len(earlier),
        [like(anchor.shape, anchor.dtype)] * 2 + [like(got[0].shape)] * inside,
        [state, state] + [part] * inside,
        grid=(capacity,),
        aliases={inside + 2: 0, inside + 3: 1} if earlier else {},
        after=after,
        name="update_chunk",
    )


def pack_for_planes(here, owner_pos, owner_used, backs, slots, after):
    capacity, _, row_count, width = backs[0].shape
    inside = len(backs)

    def kernel(here_ref, pos_ref, used_ref, *refs):
        ins, outs = refs[:inside], refs[inside:]
        for m in range(inside):
            for c in range(capacity):

                @pl.when(used_ref[m, c] > 0)
                def _(m=m, c=c):
                    for k, out in enumerate(outs):
                        out[pos_ref[m, c]] = ins[m][c, lax.rem(here_ref[1] + k, PLANES)]

    packed = (slots, row_count, width)
    return call(
        kernel,
        (here, owner_pos, owner_used),
        backs,
        [full(backs[0].shape)] * inside,
        [like(packed)] * PLANES,
        [full(packed)] * PLANES,
        after=after,
        name="pack_for_planes",
    )


def unpack(in_ids, in_counts, parts, slab_count, after):
    _, row_count, width = parts[0].shape

    def kernel(ids_ref, counts_ref, *refs):
        for k in range(PLANES):

            @pl.loop(0, counts_ref[k])
            def _(j, k=k):
                refs[-1][ids_ref[k, j]] = refs[k][j]

    block = (slab_count, row_count, width)
    return call(
        kernel,
        (in_ids, in_counts),
        parts,
        [full(parts[0].shape)] * PLANES,
        like(block),
        full(block),
        after=after,
        name="unpack",
    )


def place(here, own, other, start, whole_shape, earlier, after):
    width = own.shape[2]

    def kernel(here_ref, own_ref, other_ref, *refs):
        out_ref, done = refs[-2:]
        copies = []
        for i, (group, value) in enumerate(((here_ref[0], own_ref), (1 - here_ref[0], other_ref))):
            chosen = columns(group, out_ref, start, width)
            copies.append(pltpu.make_async_copy(value, out_ref.at[:, :, chosen], done.at[i]))
        for copy in copies:
            copy.start()
        for copy in copies:
            copy.wait()

    return call(
        kernel,
        (here,),
        (own, other, *earlier),
        [full(own.shape)] * 2 + [WHOLE] * len(earlier),
        like(whole_shape),
        WHOLE,
        aliases={2: 0} if earlier else {},
        after=after,
        scratch=[pltpu.SemaphoreType.DMA((2,))],
        name="place",
    )


def project_embed(embed_basis, anchor_embed, embed_rows, peer_rows, after):
    def kernel(basis_ref, anchor_ref, mine_ref, peer_ref, out_ref):
        total = mine_ref[...].astype(jnp.float32) + peer_ref[...].astype(jnp.float32)
        out_ref[...] = lax.dot_general(
            basis_ref[...],
            anchor_ref[...] - total * 0.5,
            (((0,), (0,)), ((), ())),
            precision=lax.Precision.HIGHEST,
            preferred_element_type=jnp.float32,
        )

    operands = (embed_basis, anchor_embed, embed_rows, peer_rows)
    shape = (embed_basis.shape[1], anchor_embed.shape[1])
    return call(
        kernel,
        (),
        operands,
        [full(value.shape) for value in operands],
        like(shape, jnp.float32),
        full(shape),
        after=after,
        name="project_embed",
    )


def add(first, second, after):
    def kernel(first_ref, second_ref, out_ref):
        out_ref[...] = first_ref[...] + second_ref[...]

    return call(
        kernel,
        (),
        (first, second),
        [full(first.shape)] * 2,
        like(first.shape, first.dtype),
        full(first.shape),
        after=after,
        name="add",
    )


def update_embed(embed_basis, embed_factor, anchor_embed, momentum_embed, after):
    def kernel(basis_ref, factor_ref, anchor_ref, moment_ref, *outs):
        embed_grad = jnp.dot(
            basis_ref[...],
            factor_ref[...],
            precision=lax.Precision.HIGHEST,
            preferred_element_type=jnp.float32,
        )
        anchor = anchor_ref[...]
        new_anchor, new_moment = nesterov(anchor, moment_ref[...], anchor - embed_grad)
        for out, value in zip(outs, (new_anchor, new_moment, new_anchor)):
            out[...] = value.astype(out.dtype)

    operands = (embed_basis, embed_factor, anchor_embed, momentum_embed)
    shape = anchor_embed.shape
    return call(
        kernel,
        (),
        operands,
        [full(value.shape) for value in operands],
        [like(shape, jnp.float32), like(shape, jnp.float32), like(shape)],
        [full(shape)] * 3,
        after=after,
        name="update_embed",
    )


def moved(
    slots,
    local_shape,
    tables,
    first_columns,
    later_columns,
    anchor,
    moment,
    embed_rows,
    peer_embed,
    anchor_embed,
    momentum_embed,
    embed_basis,
):
    here, to_ids, from_ids, from_counts, owner_pos, owner_used = tables
    devices = lax.axis_size("shard")
    inside = devices // PLANES
    capacity = anchor.shape[0]
    swap = [(0, 1), (1, 0)]

    def over_planes(parts):
        return [parts[0]] + [
            lax.ppermute(
                parts[k], "shard", [(i, (i + k * inside) % devices) for i in range(devices)]
            )
            for k in range(1, PLANES)
        ]

    def in_plane(parts):
        return [parts[0]] + [
            lax.ppermute(parts[m], "shard", [(i, i ^ m) for i in range(devices)])
            for m in range(1, inside)
        ]

    def embed_steps():
        after = yield None
        factor = project_embed(embed_basis, anchor_embed, embed_rows, peer_embed, after)
        step = 1
        while step < devices:
            pairs = [(i, i ^ step) for i in range(devices)]
            other = lax.ppermute(factor, "shard", pairs)
            after = yield factor
            factor = add(factor, other, after)
            step *= 2
        after = yield factor
        yield update_embed(embed_basis, factor, anchor_embed, momentum_embed, after)

    embed = embed_steps()
    next(embed)
    new_embed = None
    held = [
        (mine, lax.ppermute(outgoing, "group", swap)) for outgoing, mine in later_columns
    ]
    held.insert(FIRST, first_columns)
    state, new_rows, after = (), (), ()
    for chunk, step, *waits in ORDER:
        for wait in waits:
            after += tuple(held[wait])
        if chunk == EMBED:
            new_embed = embed.send(after)
            if isinstance(new_embed, jax.Array):
                after = (new_embed,)
            continue
        start = CHUNKS[chunk][0] * (local_shape[2] // 16)
        value = held[chunk]
        if step == 1:
            parts = sum_and_pack(to_ids, *value, slots, after)
            token, value = parts[0], over_planes(parts)
        elif step == 2:
            parts = pack_for_owners(here, owner_pos, value, inside, capacity, after)
            token = parts[0]
            value = in_plane(parts)
        elif step == 3:
            first, second, *parts = update_chunk(
                here, owner_used, value, anchor, moment, start, state, after
            )
            state, token, value = (first, second), parts[0], in_plane(parts)
        elif step == 4:
            parts = pack_for_planes(here, owner_pos, owner_used, value, slots, after)
            token, value = parts[0], over_planes(parts)
        elif step == 5:
            token = unpack(from_ids, from_counts, value, local_shape[0], after)
            value = (token, lax.ppermute(token, "group", swap))
        else:
            new_rows = (place(here, *value, start, local_shape, new_rows, after),)
        held[chunk] = value
        after = (token,)
    while isinstance(new_embed, jax.Array):
        new_embed = embed.send(after)
    return (*state, *new_rows, *new_embed)


def on_device(
    replica_weights,
    anchor_slabs,
    momentum_slabs,
    slab_owner,
    replica_embed,
    anchor_embed,
    momentum_embed,
    embed_basis,
):
    devices = lax.axis_size("shard")
    capacity = anchor_slabs.shape[1]
    inside = devices // PLANES
    device_here = lax.axis_index("shard")
    here = jnp.stack(
        [lax.axis_index("group"), device_here // inside, device_here % inside]
    ).astype(jnp.int32)

    local_rows, embed_rows = replica_weights[0], replica_embed[0]
    half = local_rows.shape[2] // 2
    pairs = []
    for start, width in CHUNKS:
        pairs.append(
            tuple(
                lax.dynamic_slice_in_dim(
                    local_rows, group * half + start * (half // 8), width * (half // 8), axis=2
                )
                for group in (1 - here[0], here[0])
            )
        )
    outgoing, mine = pairs.pop(FIRST)
    swap = [(0, 1), (1, 0)]
    peer = lax.ppermute(outgoing, "group", swap)
    *tables, fullest = slot_tables(here, slab_owner, devices, capacity)
    operands = (
        (here, *tables),
        (mine, peer),
        pairs,
        anchor_slabs[0],
        momentum_slabs[0],
        embed_rows,
        lax.ppermute(embed_rows, "group", swap),
        anchor_embed,
        momentum_embed,
        embed_basis,
    )
    most = capacity * inside
    fewer = most * 3 // 4
    shape = local_rows.shape
    results = lax.cond(
        fullest[0] <= fewer,
        lambda *values: moved(fewer, shape, *values),
        lambda *values: moved(most, shape, *values),
        *operands,
    )
    return tuple(
        value[None] if index not in (3, 4) else value for index, value in enumerate(results)
    )


def solution(mesh):
    in_specs = (
        P("group", None, "shard", None),
        P("shard", None, None, "group"),
        P("shard", None, None, "group"),
        P(),
        P("group", "shard", None),
        P("shard", None),
        P("shard", None),
        P("shard", None),
    )
    out_specs = (
        P("shard", None, None, "group"),
        P("shard", None, None, "group"),
        P("group", None, "shard", None),
        P("shard", None),
        P("shard", None),
        P("group", "shard", None),
    )
    return jax.shard_map(
        on_device, mesh=mesh, in_specs=in_specs, out_specs=out_specs, check_vma=False
    )
```

```python
import functools

import jax
import jax.numpy as jnp
from jax import lax
from jax.experimental import pallas as pl
from jax.experimental.pallas import tpu as pltpu
from jax.sharding import PartitionSpec as P

OUTER_RATE = 0.7
MOMENTUM_COEF = 0.9
PLANES = 4
CHUNKS = ((4, 2), (0, 4), (6, 2))
EMBED = None
FIRST = 0
PLANS = (
    (
        5,
        (
            (0, 1), (0, 2), (EMBED, 0), (1, 1), (EMBED, 0), (0, 3), (2, 1, 1), (1, 2), (0, 4), (EMBED, 0), (2, 2),
            (1, 3), (2, 3), (0, 5), (1, 4), (2, 4), (0, 6), (1, 5), (2, 5), (EMBED, 0), (2, 6), (1, 6), (EMBED, 0),
            (EMBED, 0),
        ),
    ),
    (
        6,
        (
            (EMBED, 0), (0, 1), (1, 1), (EMBED, 0), (0, 2), (0, 3), (2, 1, 1), (1, 2), (EMBED, 0), (0, 4), (2, 2),
            (1, 3), (2, 3), (0, 5), (1, 4), (2, 4, 1), (0, 6, 2), (EMBED, 0), (1, 5), (EMBED, 0), (1, 6, 2), (2, 5),
            (2, 6), (EMBED, 0),
        ),
    ),
    (
        8,
        (
            (0, 1), (1, 1, 0), (0, 2), (EMBED, 0), (0, 3), (EMBED, 0), (2, 1, 1), (1, 2), (EMBED, 0), (0, 4, 2),
            (2, 2), (1, 3), (2, 3), (0, 5), (1, 4), (2, 4, 1), (EMBED, 0), (1, 5), (0, 6), (2, 5), (EMBED, 0),
            (1, 6), (EMBED, 0), (2, 6),
        ),
    ),
)
VMEM_LIMIT = 48 * 1024 * 1024


def nesterov(anchor_value, moment, mean_value):
    outer_grad = anchor_value - mean_value
    new_moment = MOMENTUM_COEF * moment + outer_grad
    new_anchor = anchor_value - OUTER_RATE * (outer_grad + MOMENTUM_COEF * new_moment)
    return (new_anchor, new_moment)


def call(
    kernel, scalars, operands, in_specs, out_shape, out_specs, grid=(1,), aliases=None, after=(), name=None,
    scratch=()
):
    first, last = len(scalars), len(scalars) + len(after)

    def body(*refs):
        kernel(*refs[:first], *refs[last:])

    return pl.pallas_call(
        body,
        grid_spec=pltpu.PrefetchScalarGridSpec(
            num_scalar_prefetch=first,
            grid=grid,
            in_specs=[pl.BlockSpec(memory_space=pl.ANY)] * len(after) + in_specs,
            out_specs=out_specs,
            scratch_shapes=scratch,
        ),
        out_shape=out_shape,
        input_output_aliases={first + len(after) + i: o for i, o in (aliases or {}).items()},
        compiler_params=pltpu.CompilerParams(vmem_limit_bytes=VMEM_LIMIT),
        name=name,
        cost_estimate=pl.CostEstimate(flops=1, bytes_accessed=1, transcendentals=0),
    )(*scalars, *after, *operands)


def full(shape):
    return pl.BlockSpec(memory_space=pltpu.VMEM)


def like(shape, dtype=jnp.bfloat16):
    return jax.ShapeDtypeStruct(shape, dtype)


WHOLE = pl.BlockSpec(memory_space=pl.ANY)


def columns(group, rows, start, width):
    first = group * (rows.shape[2] // 2) + start
    return pl.ds(pl.multiple_of(first, width), width)


def slot_tables(here, slab_owner, devices, capacity):
    inside = devices // PLANES
    slab_count = slab_owner.shape[0]
    plane_slots = capacity * inside
    shift = inside.bit_length() - 1

    def kernel(
        here_ref, owner_ref, to_ref, from_ref, count_ref, pos_ref, used_ref, most_ref, planes, owners
    ):
        plane, place_here = here_ref[1], here_ref[2]
        for k in range(PLANES):
            planes[k] = 0

            @pl.loop(0, plane_slots)
            def _(j, k=k):
                to_ref[k, j] = 0
                from_ref[k, j] = 0

        @pl.loop(0, devices)
        def _(o):
            owners[o] = 0

        @pl.loop(0, inside)
        def _(m):
            for c in range(capacity):
                pos_ref[m, c] = 0
                used_ref[m, c] = 0

        @pl.loop(0, slab_count)
        def _(s):
            owner = owner_ref[s]
            its_plane = owner >> shift
            j, c = planes[its_plane], owners[owner]
            planes[its_plane] = j + 1
            owners[owner] = c + 1
            to_ref[(its_plane - plane) & (PLANES - 1), j] = s
            from_ref[(plane - its_plane) & (PLANES - 1), j] = s

            @pl.when(its_plane == plane)
            def _():
                m = (owner & (inside - 1)) ^ place_here
                pos_ref[m, c] = j
                used_ref[m, c] = 1

        most = planes[0]
        for k in range(PLANES):
            count_ref[k] = planes[(plane - k) & (PLANES - 1)]
            most = jnp.maximum(most, planes[k])
        most_ref[0] = most

    shapes = [(PLANES, plane_slots)] * 2 + [(PLANES,)] + [(inside, capacity)] * 2 + [(1,)]
    scalars = pl.BlockSpec(memory_space=pltpu.SMEM)
    return call(
        kernel,
        (here, slab_owner),
        (),
        [],
        [like(shape, jnp.int32) for shape in shapes],
        [scalars] * len(shapes),
        scratch=[pltpu.SMEM((PLANES,), jnp.int32), pltpu.SMEM((devices,), jnp.int32)],
        name="slot_tables",
    )


def sum_and_pack(plane_ids, mine, peer, slots, after):
    def kernel(ids_ref, mine_ref, peer_ref, *outs):
        for k, out in enumerate(outs):

            @pl.loop(0, slots)
            def _(j, k=k, out=out):
                i = ids_ref[k, j]
                out[j] = mine_ref[i] + peer_ref[i]

    packed = (slots,) + mine.shape[1:]
    return call(
        kernel,
        (plane_ids,),
        (mine, peer),
        [full(mine.shape)] * 2,
        [like(packed)] * PLANES,
        [full(packed)] * PLANES,
        after=after,
        name="sum_and_pack",
    )


def pack_for_owners(here, owner_pos, parts, inside, capacity, after):
    slots, row_count, width = parts[0].shape

    def kernel(here_ref, pos_ref, *refs):
        ins, outs = refs[:PLANES], refs[PLANES:]
        for k, part in enumerate(ins):
            z = lax.rem(here_ref[1] + PLANES - k, PLANES)
            for m, out in enumerate(outs):
                for c in range(capacity):
                    out[c, z] = part[pos_ref[m, c]]

    packed = (capacity, PLANES, row_count, width)
    return call(
        kernel,
        (here, owner_pos),
        parts,
        [full(parts[0].shape)] * PLANES,
        [like(packed)] * inside,
        [full(packed)] * inside,
        after=after,
        name="pack_for_owners",
    )


def update_chunk(here, used, got, anchor, moment, start, earlier, after):
    capacity, planes, row_count, width = got[0].shape
    inside = len(got)

    def kernel(here_ref, used_ref, *refs):
        ins, anchor_ref, moment_ref = refs[:inside], refs[inside], refs[inside + 1]
        new_anchor_ref, new_moment_ref = refs[-inside - 2], refs[-inside - 1]
        outs = refs[-inside:]
        c = pl.program_id(0)
        used_here = used_ref[0, c] > 0

        @pl.loop(0, planes)
        def _(z):
            for m in range(inside):
                first = (z * inside + (here_ref[2] ^ m)) * row_count
                rows = pl.ds(pl.multiple_of(first, row_count), row_count)
                anchor_value = anchor_ref[rows, :]
                moment_value = moment_ref[rows, :]
                mean = ins[m][c, z].astype(jnp.float32) * 0.5
                new_anchor, new_moment = nesterov(anchor_value, moment_value, mean)
                new_anchor = jnp.where(used_here, new_anchor, anchor_value)
                new_anchor_ref[rows, :] = new_anchor
                new_moment_ref[rows, :] = jnp.where(used_here, new_moment, moment_value)
                outs[m][c, z] = new_anchor.astype(outs[m].dtype)

    state = pl.BlockSpec((None, anchor.shape[1], width), lambda c, *_: (c, 0, start // width))
    part = full(got[0].shape)
    return call(
        kernel,
        (here, used),
        (*got, anchor, moment, *earlier),
        [part] * inside + [state, state] + [WHOLE] * len(earlier),
        [like(anchor.shape, anchor.dtype)] * 2 + [like(got[0].shape)] * inside,
        [state, state] + [part] * inside,
        grid=(capacity,),
        aliases={inside + 2: 0, inside + 3: 1} if earlier else {},
        after=after,
        name="update_chunk",
    )


def pack_for_planes(here, owner_pos, owner_used, backs, slots, after):
    capacity, _, row_count, width = backs[0].shape
    inside = len(backs)

    def kernel(here_ref, pos_ref, used_ref, *refs):
        ins, outs = refs[:inside], refs[inside:]
        for m in range(inside):
            for c in range(capacity):

                @pl.when(used_ref[m, c] > 0)
                def _(m=m, c=c):
                    for k, out in enumerate(outs):
                        out[pos_ref[m, c]] = ins[m][c, lax.rem(here_ref[1] + k, PLANES)]

    packed = (slots, row_count, width)
    return call(
        kernel,
        (here, owner_pos, owner_used),
        backs,
        [full(backs[0].shape)] * inside,
        [like(packed)] * PLANES,
        [full(packed)] * PLANES,
        after=after,
        name="pack_for_planes",
    )


def unpack(in_ids, in_counts, parts, slab_count, after):
    _, row_count, width = parts[0].shape

    def kernel(ids_ref, counts_ref, *refs):
        for k in range(PLANES):

            @pl.loop(0, counts_ref[k])
            def _(j, k=k):
                refs[-1][ids_ref[k, j]] = refs[k][j]

    block = (slab_count, row_count, width)
    return call(
        kernel,
        (in_ids, in_counts),
        parts,
        [full(parts[0].shape)] * PLANES,
        like(block),
        full(block),
        after=after,
        name="unpack",
    )


def place(here, own, other, start, whole_shape, earlier, after):
    width = own.shape[2]

    def kernel(here_ref, own_ref, other_ref, *refs):
        out_ref, done = refs[-2:]
        copies = []
        for i, (group, value) in enumerate(((here_ref[0], own_ref), (1 - here_ref[0], other_ref))):
            chosen = columns(group, out_ref, start, width)
            copies.append(pltpu.make_async_copy(value, out_ref.at[:, :, chosen], done.at[i]))
        for copy in copies:
            copy.start()
        for copy in copies:
            copy.wait()

    return call(
        kernel,
        (here,),
        (own, other, *earlier),
        [full(own.shape)] * 2 + [WHOLE] * len(earlier),
        like(whole_shape),
        WHOLE,
        aliases={2: 0} if earlier else {},
        after=after,
        scratch=[pltpu.SemaphoreType.DMA((2,))],
        name="place",
    )


def project_embed(embed_basis, anchor_embed, embed_rows, peer_rows, after):
    def kernel(basis_ref, anchor_ref, mine_ref, peer_ref, out_ref):
        total = mine_ref[...].astype(jnp.float32) + peer_ref[...].astype(jnp.float32)
        out_ref[...] = lax.dot_general(
            basis_ref[...],
            anchor_ref[...] - total * 0.5,
            (((0,), (0,)), ((), ())),
            precision=lax.Precision.HIGHEST,
            preferred_element_type=jnp.float32,
        )

    operands = (embed_basis, anchor_embed, embed_rows, peer_rows)
    shape = (embed_basis.shape[1], anchor_embed.shape[1])
    return call(
        kernel,
        (),
        operands,
        [full(value.shape) for value in operands],
        like(shape, jnp.float32),
        full(shape),
        after=after,
        name="project_embed",
    )


def add(first, second, after):
    def kernel(first_ref, second_ref, out_ref):
        out_ref[...] = first_ref[...] + second_ref[...]

    return call(
        kernel,
        (),
        (first, second),
        [full(first.shape)] * 2,
        like(first.shape, first.dtype),
        full(first.shape),
        after=after,
        name="add",
    )


def update_embed(embed_basis, embed_factor, anchor_embed, momentum_embed, after):
    def kernel(basis_ref, factor_ref, anchor_ref, moment_ref, *outs):
        embed_grad = jnp.dot(
            basis_ref[...],
            factor_ref[...],
            precision=lax.Precision.HIGHEST,
            preferred_element_type=jnp.float32,
        )
        anchor = anchor_ref[...]
        new_anchor, new_moment = nesterov(anchor, moment_ref[...], anchor - embed_grad)
        for out, value in zip(outs, (new_anchor, new_moment, new_anchor)):
            out[...] = value.astype(out.dtype)

    operands = (embed_basis, embed_factor, anchor_embed, momentum_embed)
    shape = anchor_embed.shape
    return call(
        kernel,
        (),
        operands,
        [full(value.shape) for value in operands],
        [like(shape, jnp.float32), like(shape, jnp.float32), like(shape)],
        [full(shape)] * 3,
        after=after,
        name="update_embed",
    )


def moved(
    slots,
    order,
    local_shape,
    tables,
    first_columns,
    later_columns,
    anchor,
    moment,
    embed_rows,
    peer_embed,
    anchor_embed,
    momentum_embed,
    embed_basis,
):
    here, to_ids, from_ids, from_counts, owner_pos, owner_used = tables
    devices = lax.axis_size("shard")
    inside = devices // PLANES
    capacity = anchor.shape[0]
    swap = [(0, 1), (1, 0)]

    def over_planes(parts):
        return [parts[0]] + [
            lax.ppermute(
                parts[k], "shard", [(i, (i + k * inside) % devices) for i in range(devices)]
            )
            for k in range(1, PLANES)
        ]

    def in_plane(parts):
        return [parts[0]] + [
            lax.ppermute(parts[m], "shard", [(i, i ^ m) for i in range(devices)])
            for m in range(1, inside)
        ]

    def embed_steps():
        after = yield None
        factor = project_embed(embed_basis, anchor_embed, embed_rows, peer_embed, after)
        step = 1
        while step < devices:
            pairs = [(i, i ^ step) for i in range(devices)]
            other = lax.ppermute(factor, "shard", pairs)
            after = yield factor
            factor = add(factor, other, after)
            step *= 2
        after = yield factor
        yield update_embed(embed_basis, factor, anchor_embed, momentum_embed, after)

    embed = embed_steps()
    next(embed)
    new_embed = None
    held = [
        (mine, lax.ppermute(outgoing, "group", swap)) for outgoing, mine in later_columns
    ]
    held.insert(FIRST, first_columns)
    state, new_rows, after = (), (), ()
    for chunk, step, *waits in order:
        for wait in waits:
            after += tuple(held[wait])
        if chunk == EMBED:
            new_embed = embed.send(after)
            if isinstance(new_embed, jax.Array):
                after = (new_embed,)
            continue
        start = CHUNKS[chunk][0] * (local_shape[2] // 16)
        value = held[chunk]
        if step == 1:
            parts = sum_and_pack(to_ids, *value, slots, after)
            token, value = parts[0], over_planes(parts)
        elif step == 2:
            parts = pack_for_owners(here, owner_pos, value, inside, capacity, after)
            token = parts[0]
            value = in_plane(parts)
        elif step == 3:
            first, second, *parts = update_chunk(
                here, owner_used, value, anchor, moment, start, state, after
            )
            state, token, value = (first, second), parts[0], in_plane(parts)
        elif step == 4:
            parts = pack_for_planes(here, owner_pos, owner_used, value, slots, after)
            token, value = parts[0], over_planes(parts)
        elif step == 5:
            token = unpack(from_ids, from_counts, value, local_shape[0], after)
            value = (token, lax.ppermute(token, "group", swap))
        else:
            new_rows = (place(here, *value, start, local_shape, new_rows, after),)
        held[chunk] = value
        after = (token,)
    while isinstance(new_embed, jax.Array):
        new_embed = embed.send(after)
    return (*state, *new_rows, *new_embed)


def on_device(
    replica_weights,
    anchor_slabs,
    momentum_slabs,
    slab_owner,
    replica_embed,
    anchor_embed,
    momentum_embed,
    embed_basis,
):
    devices = lax.axis_size("shard")
    capacity = anchor_slabs.shape[1]
    inside = devices // PLANES
    device_here = lax.axis_index("shard")
    here = jnp.stack(
        [lax.axis_index("group"), device_here // inside, device_here % inside]
    ).astype(jnp.int32)

    local_rows, embed_rows = replica_weights[0], replica_embed[0]
    half = local_rows.shape[2] // 2
    pairs = []
    for start, width in CHUNKS:
        pairs.append(
            tuple(
                lax.dynamic_slice_in_dim(
                    local_rows, group * half + start * (half // 8), width * (half // 8), axis=2
                )
                for group in (1 - here[0], here[0])
            )
        )
    outgoing, mine = pairs.pop(FIRST)
    swap = [(0, 1), (1, 0)]
    peer = lax.ppermute(outgoing, "group", swap)
    *tables, fullest = slot_tables(here, slab_owner, devices, capacity)
    mine, pairs = lax.optimization_barrier((mine, pairs))
    operands = (
        (here, *tables),
        (mine, peer),
        pairs,
        anchor_slabs[0],
        momentum_slabs[0],
        embed_rows,
        lax.ppermute(embed_rows, "group", swap),
        anchor_embed,
        momentum_embed,
        embed_basis,
    )
    most, shape = capacity * inside, local_rows.shape
    counts = [most * eighths // 8 for eighths, _ in PLANS]
    results = lax.switch(
        sum((fullest[0] > count).astype(jnp.int32) for count in counts[:-1]),
        [functools.partial(moved, n, order, shape) for n, (_, order) in zip(counts, PLANS)],
        *operands,
    )
    return tuple(
        value[None] if index not in (3, 4) else value for index, value in enumerate(results)
    )


def solution(mesh):
    in_specs = (
        P("group", None, "shard", None),
        P("shard", None, None, "group"),
        P("shard", None, None, "group"),
        P(),
        P("group", "shard", None),
        P("shard", None),
        P("shard", None),
        P("shard", None),
    )
    out_specs = (
        P("shard", None, None, "group"),
        P("shard", None, None, "group"),
        P("group", None, "shard", None),
        P("shard", None),
        P("shard", None),
        P("group", "shard", None),
    )
    return jax.shard_map(
        on_device, mesh=mesh, in_specs=in_specs, out_specs=out_specs, check_vma=False
    )
```

```python
import functools

import jax
import jax.numpy as jnp
from jax import lax
from jax.experimental import pallas as pl
from jax.experimental.pallas import tpu as pltpu
from jax.sharding import PartitionSpec as P

OUTER_RATE = 0.7
MOMENTUM_COEF = 0.9
PLANES = 4
CHUNKS = ((4, 2), (0, 4), (6, 2))
EMBED = None
FIRST = 0
PLANS = (
    (
        5,
        (
            (0, 1), (0, 2), (EMBED, 0), (1, 1), (EMBED, 0), (0, 3), (2, 1, 1), (1, 2), (0, 4), (EMBED, 0), (2, 2),
            (1, 3), (2, 3), (0, 5), (1, 4), (2, 4), (0, 6), (1, 5), (2, 5), (EMBED, 0), (2, 6), (1, 6), (EMBED, 0),
            (EMBED, 0),
        ),
    ),
    (
        6,
        (
            (0, 1), (1, 1, 0), (0, 2), (0, 3), (2, 1), (1, 2), (0, 4), (2, 2), (1, 3), (2, 3), (0, 5, 1),
            (EMBED, 0), (1, 4), (0, 6, 1), (2, 4), (EMBED, 0), (EMBED, 0), (1, 5), (2, 5), (EMBED, 0), (EMBED, 0),
            (EMBED, 0), (2, 6), (1, 6),
        ),
    ),
    (
        8,
        (
            (0, 1), (1, 1, 0), (0, 2), (EMBED, 0), (0, 3), (2, 1, 1), (1, 2), (0, 4, 2), (EMBED, 0), (2, 2), (1, 3),
            (2, 3), (0, 5), (1, 4), (2, 4), (EMBED, 0), (1, 5), (2, 5), (0, 6), (EMBED, 0), (EMBED, 0), (1, 6),
            (2, 6), (EMBED, 0),
        ),
    ),
)
VMEM_LIMIT = 48 * 1024 * 1024


def nesterov(anchor_value, moment, mean_value):
    outer_grad = anchor_value - mean_value
    new_moment = MOMENTUM_COEF * moment + outer_grad
    new_anchor = anchor_value - OUTER_RATE * (outer_grad + MOMENTUM_COEF * new_moment)
    return (new_anchor, new_moment)


def call(
    kernel, scalars, operands, in_specs, out_shape, out_specs, grid=(1,), aliases=None, after=(), name=None,
    scratch=()
):
    first, last = len(scalars), len(scalars) + len(after)

    def body(*refs):
        kernel(*refs[:first], *refs[last:])

    return pl.pallas_call(
        body,
        grid_spec=pltpu.PrefetchScalarGridSpec(
            num_scalar_prefetch=first,
            grid=grid,
            in_specs=[pl.BlockSpec(memory_space=pl.ANY)] * len(after) + in_specs,
            out_specs=out_specs,
            scratch_shapes=scratch,
        ),
        out_shape=out_shape,
        input_output_aliases={first + len(after) + i: o for i, o in (aliases or {}).items()},
        compiler_params=pltpu.CompilerParams(vmem_limit_bytes=VMEM_LIMIT),
        name=name,
        cost_estimate=pl.CostEstimate(flops=1, bytes_accessed=1, transcendentals=0),
    )(*scalars, *after, *operands)


def full(shape):
    return pl.BlockSpec(memory_space=pltpu.VMEM)


def like(shape, dtype=jnp.bfloat16):
    return jax.ShapeDtypeStruct(shape, dtype)


WHOLE = pl.BlockSpec(memory_space=pl.ANY)


def columns(group, rows, start, width):
    first = group * (rows.shape[2] // 2) + start
    return pl.ds(pl.multiple_of(first, width), width)


def slot_tables(here, slab_owner, devices, capacity):
    inside = devices // PLANES
    slab_count = slab_owner.shape[0]
    plane_slots = capacity * inside
    shift = inside.bit_length() - 1

    def kernel(
        here_ref, owner_ref, to_ref, from_ref, count_ref, pos_ref, used_ref, most_ref, planes, owners
    ):
        plane, place_here = here_ref[1], here_ref[2]
        for k in range(PLANES):
            planes[k] = 0

            @pl.loop(0, plane_slots)
            def _(j, k=k):
                to_ref[k, j] = 0
                from_ref[k, j] = 0

        @pl.loop(0, devices)
        def _(o):
            owners[o] = 0

        @pl.loop(0, inside)
        def _(m):
            for c in range(capacity):
                pos_ref[m, c] = 0
                used_ref[m, c] = 0

        @pl.loop(0, slab_count)
        def _(s):
            owner = owner_ref[s]
            its_plane = owner >> shift
            j, c = planes[its_plane], owners[owner]
            planes[its_plane] = j + 1
            owners[owner] = c + 1
            to_ref[(its_plane - plane) & (PLANES - 1), j] = s
            from_ref[(plane - its_plane) & (PLANES - 1), j] = s

            @pl.when(its_plane == plane)
            def _():
                m = (owner & (inside - 1)) ^ place_here
                pos_ref[m, c] = j
                used_ref[m, c] = 1

        most = planes[0]
        for k in range(PLANES):
            count_ref[k] = planes[(plane - k) & (PLANES - 1)]
            most = jnp.maximum(most, planes[k])
        most_ref[0] = most

    shapes = [(PLANES, plane_slots)] * 2 + [(PLANES,)] + [(inside, capacity)] * 2 + [(1,)]
    scalars = pl.BlockSpec(memory_space=pltpu.SMEM)
    return call(
        kernel,
        (here, slab_owner),
        (),
        [],
        [like(shape, jnp.int32) for shape in shapes],
        [scalars] * len(shapes),
        scratch=[pltpu.SMEM((PLANES,), jnp.int32), pltpu.SMEM((devices,), jnp.int32)],
        name="slot_tables",
    )


def sum_and_pack(plane_ids, mine, peer, slots, after):
    def kernel(ids_ref, mine_ref, peer_ref, *outs):
        for k, out in enumerate(outs):

            @pl.loop(0, slots)
            def _(j, k=k, out=out):
                i = ids_ref[k, j]
                out[j] = mine_ref[i] + peer_ref[i]

    packed = (slots,) + mine.shape[1:]
    return call(
        kernel,
        (plane_ids,),
        (mine, peer),
        [full(mine.shape)] * 2,
        [like(packed)] * PLANES,
        [full(packed)] * PLANES,
        after=after,
        name="sum_and_pack",
    )


def pack_for_owners(here, owner_pos, parts, inside, capacity, after):
    slots, row_count, width = parts[0].shape

    def kernel(here_ref, pos_ref, *refs):
        ins, outs = refs[:PLANES], refs[PLANES:]
        for k, part in enumerate(ins):
            z = lax.rem(here_ref[1] + PLANES - k, PLANES)
            for m, out in enumerate(outs):
                for c in range(capacity):
                    out[c, z] = part[pos_ref[m, c]]

    packed = (capacity, PLANES, row_count, width)
    return call(
        kernel,
        (here, owner_pos),
        parts,
        [full(parts[0].shape)] * PLANES,
        [like(packed)] * inside,
        [full(packed)] * inside,
        after=after,
        name="pack_for_owners",
    )


def update_chunk(here, used, got, anchor, moment, start, earlier, after):
    capacity, planes, row_count, width = got[0].shape
    inside = len(got)

    def kernel(here_ref, used_ref, *refs):
        ins, anchor_ref, moment_ref = refs[:inside], refs[inside], refs[inside + 1]
        new_anchor_ref, new_moment_ref = refs[-inside - 2], refs[-inside - 1]
        outs = refs[-inside:]
        c = pl.program_id(0)
        used_here = used_ref[0, c] > 0

        @pl.loop(0, planes)
        def _(z):
            for m in range(inside):
                first = (z * inside + (here_ref[2] ^ m)) * row_count
                rows = pl.ds(pl.multiple_of(first, row_count), row_count)
                anchor_value = anchor_ref[rows, :]
                moment_value = moment_ref[rows, :]
                mean = ins[m][c, z].astype(jnp.float32) * 0.5
                new_anchor, new_moment = nesterov(anchor_value, moment_value, mean)
                new_anchor = jnp.where(used_here, new_anchor, anchor_value)
                new_anchor_ref[rows, :] = new_anchor
                new_moment_ref[rows, :] = jnp.where(used_here, new_moment, moment_value)
                outs[m][c, z] = new_anchor.astype(outs[m].dtype)

    state = pl.BlockSpec((None, anchor.shape[1], width), lambda c, *_: (c, 0, start // width))
    part = full(got[0].shape)
    return call(
        kernel,
        (here, used),
        (*got, anchor, moment, *earlier),
        [part] * inside + [state, state] + [WHOLE] * len(earlier),
        [like(anchor.shape, anchor.dtype)] * 2 + [like(got[0].shape)] * inside,
        [state, state] + [part] * inside,
        grid=(capacity,),
        aliases={inside + 2: 0, inside + 3: 1} if earlier else {},
        after=after,
        name="update_chunk",
    )


def pack_for_planes(here, owner_pos, owner_used, backs, slots, after):
    capacity, _, row_count, width = backs[0].shape
    inside = len(backs)

    def kernel(here_ref, pos_ref, used_ref, *refs):
        ins, outs = refs[:inside], refs[inside:]
        for m in range(inside):
            for c in range(capacity):

                @pl.when(used_ref[m, c] > 0)
                def _(m=m, c=c):
                    for k, out in enumerate(outs):
                        out[pos_ref[m, c]] = ins[m][c, lax.rem(here_ref[1] + k, PLANES)]

    packed = (slots, row_count, width)
    return call(
        kernel,
        (here, owner_pos, owner_used),
        backs,
        [full(backs[0].shape)] * inside,
        [like(packed)] * PLANES,
        [full(packed)] * PLANES,
        after=after,
        name="pack_for_planes",
    )


def unpack(in_ids, in_counts, parts, slab_count, after):
    _, row_count, width = parts[0].shape

    def kernel(ids_ref, counts_ref, *refs):
        for k in range(PLANES):

            @pl.loop(0, counts_ref[k])
            def _(j, k=k):
                refs[-1][ids_ref[k, j]] = refs[k][j]

    block = (slab_count, row_count, width)
    return call(
        kernel,
        (in_ids, in_counts),
        parts,
        [full(parts[0].shape)] * PLANES,
        like(block),
        full(block),
        after=after,
        name="unpack",
    )


def place(here, own, other, start, whole_shape, earlier, after):
    width = own.shape[2]

    def kernel(here_ref, own_ref, other_ref, *refs):
        out_ref, done = refs[-2:]
        copies = []
        for i, (group, value) in enumerate(((here_ref[0], own_ref), (1 - here_ref[0], other_ref))):
            chosen = columns(group, out_ref, start, width)
            copies.append(pltpu.make_async_copy(value, out_ref.at[:, :, chosen], done.at[i]))
        for copy in copies:
            copy.start()
        for copy in copies:
            copy.wait()

    return call(
        kernel,
        (here,),
        (own, other, *earlier),
        [full(own.shape)] * 2 + [WHOLE] * len(earlier),
        like(whole_shape),
        WHOLE,
        aliases={2: 0} if earlier else {},
        after=after,
        scratch=[pltpu.SemaphoreType.DMA((2,))],
        name="place",
    )


def project_embed(embed_basis, anchor_embed, embed_rows, peer_rows, after):
    def kernel(basis_ref, anchor_ref, mine_ref, peer_ref, out_ref):
        total = mine_ref[...].astype(jnp.float32) + peer_ref[...].astype(jnp.float32)
        out_ref[...] = lax.dot_general(
            basis_ref[...],
            anchor_ref[...] - total * 0.5,
            (((0,), (0,)), ((), ())),
            precision=lax.Precision.HIGHEST,
            preferred_element_type=jnp.float32,
        )

    operands = (embed_basis, anchor_embed, embed_rows, peer_rows)
    shape = (embed_basis.shape[1], anchor_embed.shape[1])
    return call(
        kernel,
        (),
        operands,
        [full(value.shape) for value in operands],
        like(shape, jnp.float32),
        full(shape),
        after=after,
        name="project_embed",
    )


def add(first, second, after):
    def kernel(first_ref, second_ref, out_ref):
        out_ref[...] = first_ref[...] + second_ref[...]

    return call(
        kernel,
        (),
        (first, second),
        [full(first.shape)] * 2,
        like(first.shape, first.dtype),
        full(first.shape),
        after=after,
        name="add",
    )


def update_embed(embed_basis, embed_factor, anchor_embed, momentum_embed, after):
    def kernel(basis_ref, factor_ref, anchor_ref, moment_ref, *outs):
        embed_grad = jnp.dot(
            basis_ref[...],
            factor_ref[...],
            precision=lax.Precision.HIGHEST,
            preferred_element_type=jnp.float32,
        )
        anchor = anchor_ref[...]
        new_anchor, new_moment = nesterov(anchor, moment_ref[...], anchor - embed_grad)
        for out, value in zip(outs, (new_anchor, new_moment, new_anchor)):
            out[...] = value.astype(out.dtype)

    operands = (embed_basis, embed_factor, anchor_embed, momentum_embed)
    shape = anchor_embed.shape
    return call(
        kernel,
        (),
        operands,
        [full(value.shape) for value in operands],
        [like(shape, jnp.float32), like(shape, jnp.float32), like(shape)],
        [full(shape)] * 3,
        after=after,
        name="update_embed",
    )


def moved(
    slots,
    order,
    local_shape,
    tables,
    first_columns,
    later_columns,
    anchor,
    moment,
    embed_rows,
    peer_embed,
    anchor_embed,
    momentum_embed,
    embed_basis,
):
    here, to_ids, from_ids, from_counts, owner_pos, owner_used = tables
    devices = lax.axis_size("shard")
    inside = devices // PLANES
    capacity = anchor.shape[0]
    swap = [(0, 1), (1, 0)]

    def over_planes(parts):
        return [parts[0]] + [
            lax.ppermute(
                parts[k], "shard", [(i, (i + k * inside) % devices) for i in range(devices)]
            )
            for k in range(1, PLANES)
        ]

    def in_plane(parts):
        return [parts[0]] + [
            lax.ppermute(parts[m], "shard", [(i, i ^ m) for i in range(devices)])
            for m in range(1, inside)
        ]

    def embed_steps():
        after = yield None
        factor = project_embed(embed_basis, anchor_embed, embed_rows, peer_embed, after)
        step = 1
        while step < devices:
            pairs = [(i, i ^ step) for i in range(devices)]
            other = lax.ppermute(factor, "shard", pairs)
            after = yield factor
            factor = add(factor, other, after)
            step *= 2
        after = yield factor
        yield update_embed(embed_basis, factor, anchor_embed, momentum_embed, after)

    embed = embed_steps()
    next(embed)
    new_embed = None
    held = [
        (mine, lax.ppermute(outgoing, "group", swap)) for outgoing, mine in later_columns
    ]
    held.insert(FIRST, first_columns)
    state, new_rows, after = (), (), ()
    for chunk, step, *waits in order:
        for wait in waits:
            after += tuple(held[wait])
        if chunk == EMBED:
            new_embed = embed.send(after)
            if isinstance(new_embed, jax.Array):
                after = (new_embed,)
            continue
        start = CHUNKS[chunk][0] * (local_shape[2] // 16)
        value = held[chunk]
        if step == 1:
            parts = sum_and_pack(to_ids, *value, slots, after)
            token, value = parts[0], over_planes(parts)
        elif step == 2:
            parts = pack_for_owners(here, owner_pos, value, inside, capacity, after)
            token = parts[0]
            value = in_plane(parts)
        elif step == 3:
            first, second, *parts = update_chunk(
                here, owner_used, value, anchor, moment, start, state, after
            )
            state, token, value = (first, second), parts[0], in_plane(parts)
        elif step == 4:
            parts = pack_for_planes(here, owner_pos, owner_used, value, slots, after)
            token, value = parts[0], over_planes(parts)
        elif step == 5:
            token = unpack(from_ids, from_counts, value, local_shape[0], after)
            value = (token, lax.ppermute(token, "group", swap))
        else:
            new_rows = (place(here, *value, start, local_shape, new_rows, after),)
        held[chunk] = value
        after = (token,)
    while isinstance(new_embed, jax.Array):
        new_embed = embed.send(after)
    return (*state, *new_rows, *new_embed)


def on_device(
    replica_weights,
    anchor_slabs,
    momentum_slabs,
    slab_owner,
    replica_embed,
    anchor_embed,
    momentum_embed,
    embed_basis,
):
    devices = lax.axis_size("shard")
    capacity = anchor_slabs.shape[1]
    inside = devices // PLANES
    device_here = lax.axis_index("shard")
    here = jnp.stack(
        [lax.axis_index("group"), device_here // inside, device_here % inside]
    ).astype(jnp.int32)

    local_rows, embed_rows = replica_weights[0], replica_embed[0]
    half = local_rows.shape[2] // 2
    pairs = []
    for start, width in CHUNKS:
        pairs.append(
            tuple(
                lax.dynamic_slice_in_dim(
                    local_rows, group * half + start * (half // 8), width * (half // 8), axis=2
                )
                for group in (1 - here[0], here[0])
            )
        )
    outgoing, mine = pairs.pop(FIRST)
    swap = [(0, 1), (1, 0)]
    peer = lax.ppermute(outgoing, "group", swap)
    *tables, fullest = slot_tables(here, slab_owner, devices, capacity)
    mine, pairs = lax.optimization_barrier((mine, pairs))
    operands = (
        (here, *tables),
        (mine, peer),
        pairs,
        anchor_slabs[0],
        momentum_slabs[0],
        embed_rows,
        lax.ppermute(embed_rows, "group", swap),
        anchor_embed,
        momentum_embed,
        embed_basis,
    )
    most, shape = capacity * inside, local_rows.shape
    counts = [most * eighths // 8 for eighths, _ in PLANS]
    results = lax.switch(
        sum((fullest[0] > count).astype(jnp.int32) for count in counts[:-1]),
        [functools.partial(moved, n, order, shape) for n, (_, order) in zip(counts, PLANS)],
        *operands,
    )
    return tuple(
        value[None] if index not in (3, 4) else value for index, value in enumerate(results)
    )


def solution(mesh):
    in_specs = (
        P("group", None, "shard", None),
        P("shard", None, None, "group"),
        P("shard", None, None, "group"),
        P(),
        P("group", "shard", None),
        P("shard", None),
        P("shard", None),
        P("shard", None),
    )
    out_specs = (
        P("shard", None, None, "group"),
        P("shard", None, None, "group"),
        P("group", None, "shard", None),
        P("shard", None),
        P("shard", None),
        P("group", "shard", None),
    )
    return jax.shard_map(
        on_device, mesh=mesh, in_specs=in_specs, out_specs=out_specs, check_vma=False
    )
```
